32 devices in a mesh: gx: 8 (over y, x, core), yz: 4 (over z).
Axes of the slice: x: 2, y: 2, z: 4, core: 2. Of those that a mesh axis runs over, the one named last changes fastest.
Arguments:
- vectors: float32 [8, 128, 64, 512], P(None, 'gx', 'yz'), may hold values from -4 to 4
- classes: int32 [128, 64, 512], P('gx', 'yz'), may hold values from 0 to 3
- permittivity: float32 [4], replicated, may hold values from 0.01 to 10
Outputs:
- applied: float32 [8, 128, 64, 512], P(None, 'gx', 'yz')
- coarse: float32 [256, 256], P('gx', 'yz')
The draws below stay inside these ranges and needn't reach their ends.
All inputs are finite; a program needn't handle non-finite values.
Results may differ from the reference program's by a relative error of at most 0.000071.
Values sent between devices are 32-bit elements; how exact they have to be, the bound alone decides.
A program may use at most 64 MiB of HBM per device.

```python
import math
import jax
import jax.numpy as jnp
from jax import lax

K = 8
NCLASS = 4
CX = 16
CZ = 16
NY = 512
NX = 128
NZ = 64


def draw_vectors(key, part):
    key = jax.random.fold_in(key, 11)
    first_key, second_key = jax.random.split(key, 2)
    segment = NY // 8
    level_shape = (K, NX // CX, NZ // CZ, 8)
    level = jax.random.uniform(first_key, level_shape, jnp.float32, -2.0, 2.0)
    noise = 0.5 * jax.random.truncated_normal(second_key, -3.0, 3.0, (K, NX, NZ, NY), jnp.float32)
    level = jnp.repeat(jnp.repeat(jnp.repeat(level, CX, axis=1), CZ, axis=2), segment, axis=3)
    return (level + noise).astype(jnp.float32)


def place_ends(drawn, key, low, largest):
    shape = drawn.shape
    index_at = [jax.random.randint(jax.random.fold_in(key, axis), (), 0, shape[axis]) for axis in range(len(shape))]
    drawn = drawn.at[tuple(index_at)].set(low)
    longest = shape.index(max(shape))
    index_at[longest] = (index_at[longest] + 1) % shape[longest]
    return drawn.at[tuple(index_at)].set(largest)


def setup_inputs(seed: int = 0) -> dict:
    keys = jax.random.split(jax.random.key(seed), 4)
    vectors = draw_vectors(jax.random.fold_in(keys[3], 71), 0)
    classes = place_ends(jax.random.randint(keys[1], (NX, NZ, NY), 0, NCLASS), jax.random.fold_in(keys[1], 1), 0, NCLASS - 1).astype(jnp.int32)
    permittivity = jnp.clip(jnp.exp(jax.random.uniform(keys[2], (NCLASS,), jnp.float32, math.log(0.01), math.log(10.0))), 0.01, 10.0)
    return {"vectors": vectors, "classes": classes, "permittivity": permittivity}


def permit(classes, permittivity):
    onehot = (classes[..., None] == jnp.arange(permittivity.shape[0], dtype=jnp.int32)).astype(jnp.float32)
    return jnp.sum(onehot * permittivity, axis=-1)


def harmonic(first_value, second_value):
    return 2.0 * first_value * second_value / (first_value + second_value)


def reference(vectors, classes, permittivity):
    highest = lax.Precision.HIGHEST
    vector_count = vectors.shape[0]
    x_blocks = NX // CX
    z_blocks = NZ // CZ
    epsilon = permit(classes, permittivity)
    face_x = harmonic(epsilon[:-1], epsilon[1:])
    face_z = harmonic(epsilon[:, :-1], epsilon[:, 1:])
    face_y = harmonic(epsilon[:, :, :-1], epsilon[:, :, 1:])
    keep_x = ((jnp.arange(NX - 1) + 1) % CX != 0).astype(jnp.float32)[:, None, None]
    keep_z = ((jnp.arange(NZ - 1) + 1) % CZ != 0).astype(jnp.float32)[None, :, None]
    applied = jnp.zeros_like(vectors)
    applied = applied.at[:, :-1].add(face_x * (vectors[:, :-1] - keep_x * vectors[:, 1:]))
    applied = applied.at[:, 1:].add(face_x * (vectors[:, 1:] - keep_x * vectors[:, :-1]))
    applied = applied.at[:, :, :-1].add(face_z * (vectors[:, :, :-1] - keep_z * vectors[:, :, 1:]))
    applied = applied.at[:, :, 1:].add(face_z * (vectors[:, :, 1:] - keep_z * vectors[:, :, :-1]))
    applied = applied.at[:, :, :, :-1].add(face_y * (vectors[:, :, :, :-1] - vectors[:, :, :, 1:]))
    applied = applied.at[:, :, :, 1:].add(face_y * (vectors[:, :, :, 1:] - vectors[:, :, :, :-1]))
    shaped = (vector_count, x_blocks, CX, z_blocks, CZ, NY)
    self_block = jnp.einsum("kaibjy,laibjy->abkl", vectors.reshape(shaped), applied.reshape(shaped), precision=highest)
    left_face = vectors[:, CX - 1:NX - 1:CX] * face_x[CX - 1::CX]
    right_face = vectors[:, CX:NX:CX]
    xshape = (vector_count, x_blocks - 1, z_blocks, CZ, NY)
    upper_x = -jnp.einsum("kabjy,labjy->abkl", left_face.reshape(xshape), right_face.reshape(xshape), precision=highest)
    low_face = vectors[:, :, CZ - 1:NZ - 1:CZ] * face_z[:, CZ - 1::CZ]
    high_face = vectors[:, :, CZ:NZ:CZ]
    zshape = (vector_count, x_blocks, CX, z_blocks - 1, NY)
    upper_z = -jnp.einsum("kaiby,laiby->abkl", low_face.reshape(zshape), high_face.reshape(zshape), precision=highest)
    coarse_full = jnp.zeros((x_blocks, z_blocks, vector_count, x_blocks, z_blocks, vector_count), jnp.float32)
    index_a, index_b = jnp.meshgrid(jnp.arange(x_blocks), jnp.arange(z_blocks), indexing="ij")
    coarse_full = coarse_full.at[index_a, index_b, :, index_a, index_b, :].set(self_block)
    index_a, index_b = jnp.meshgrid(jnp.arange(x_blocks - 1), jnp.arange(z_blocks), indexing="ij")
    coarse_full = coarse_full.at[index_a, index_b, :, index_a + 1, index_b, :].set(upper_x)
    coarse_full = coarse_full.at[index_a + 1, index_b, :, index_a, index_b, :].set(jnp.swapaxes(upper_x, -1, -2))
    index_a, index_b = jnp.meshgrid(jnp.arange(x_blocks), jnp.arange(z_blocks - 1), indexing="ij")
    coarse_full = coarse_full.at[index_a, index_b, :, index_a, index_b + 1, :].set(upper_z)
    coarse_full = coarse_full.at[index_a, index_b + 1, :, index_a, index_b, :].set(jnp.swapaxes(upper_z, -1, -2))
    order_total = vector_count * x_blocks * z_blocks
    coarse = coarse_full.reshape(order_total, order_total) / (CZ * NY)
    return applied, coarse
```

```python
import functools

import jax
import jax.numpy as jnp
from jax import lax
from jax.experimental import pallas as pl
from jax.experimental.pallas import tpu as pltpu
from jax.sharding import PartitionSpec as P

MESH = pl.DeviceIdType.MESH
LANES = 128


def permit(classes, permittivity):
    value = jnp.full(classes.shape, permittivity[0], jnp.float32)
    for index in range(1, permittivity.shape[0]):
        value = jnp.where(classes == index, permittivity[index], value)
    return value


def harmonic(first_value, second_value):
    return 2.0 * first_value * second_value / (first_value + second_value)


def split(value):
    high = value.astype(jnp.bfloat16)
    return high, (value - high.astype(jnp.float32)).astype(jnp.bfloat16)


def contract(left, right):
    return lax.dot_general(
        left, right, (((1,), (1,)), ((), ())), preferred_element_type=jnp.float32
    )


def store_split(target, row, value):
    rows = target.shape[0] // 2
    size = value.shape[0]
    high, low = split(value)
    target[row:row + size] = high
    target[rows + row:rows + row + size] = low


def fold(product):
    rows, columns = product.shape[0] // 2, product.shape[1] // 2
    return (
        product[:rows, :columns]
        + product[:rows, columns:]
        + product[rows:, :columns]
        + product[rows:, columns:]
    )


def kernel(
    nx, nz, v_hbm, c_hbm, permittivity, applied, coarse,
    v, c, eps, c_face, v_face, c_halo, v_halo,
    left_0, right_0, left_1, right_1, total, blocks, select, strip, rows,
    load_sem, c_send, c_recv, v_send, v_recv, strip_send, strip_recv,
):
    a, b = lax.axis_index("gx"), lax.axis_index("yz")
    count, cx, cz, ny = v.shape
    width = strip.shape[2]
    neighbour = ((a - 1, b), (a + 1, b), (a, b - 1), (a, b + 1))
    present = (a > 0, a < nx - 1, b > 0, b < nz - 1)

    load_c = pltpu.make_async_copy(c_hbm, c, load_sem.at[0])
    load_v = pltpu.make_async_copy(v_hbm, v, load_sem.at[1])
    load_c.start()
    load_v.start()

    barrier = pltpu.get_barrier_semaphore()
    for face in range(2):
        @pl.when(present[face])
        def _():
            pl.semaphore_signal(barrier, inc=1, device_id=neighbour[face], device_id_type=MESH)
    for step in range(1, nz):
        pl.semaphore_signal(
            barrier, inc=1, device_id=(a, lax.rem(b + step, nz)), device_id_type=MESH
        )
    partners = (a > 0).astype(jnp.int32) + (a < nx - 1).astype(jnp.int32) + (nz - 1)

    def copies(face, source, halo, send, recv):
        return pltpu.make_async_remote_copy(
            src_ref=source, dst_ref=halo.at[face ^ 1], send_sem=send.at[face],
            recv_sem=recv.at[face ^ 1], device_id=neighbour[face], device_id_type=MESH,
        )

    def arrival(face, source, halo, send, recv):
        return pltpu.make_async_remote_copy(
            src_ref=source, dst_ref=halo.at[face], send_sem=send.at[face],
            recv_sem=recv.at[face], device_id=neighbour[face], device_id_type=MESH,
        )

    ends = (0, cx - 1, 0, cz - 1)
    c_source = tuple(c_hbm.at[ends[f]] if f < 2 else c_face.at[f - 2] for f in range(4))
    v_source = tuple(v_hbm.at[:, ends[f]] if f < 2 else v_face.at[f - 2] for f in range(4))

    load_c.wait()
    for face in (2, 3):
        c_face[face - 2] = c[:, ends[face], :]
    load_v.wait()
    for face in (2, 3):
        for k in range(count):
            v_face[face - 2, k] = v[k, :, ends[face], :]

    pl.semaphore_wait(barrier, partners)
    for face in (2, 3, 0, 1):
        @pl.when(present[face])
        def _():
            copies(face, c_source[face], c_halo, c_send, c_recv).start()
    for face in (2, 3, 0, 1):
        @pl.when(present[face])
        def _():
            copies(face, v_source[face], v_halo, v_send, v_recv).start()

    for face in range(4):
        @pl.when(jnp.logical_not(present[face]))
        def _():
            c_halo[face] = jnp.zeros(c_halo.shape[1:], jnp.int32)
            v_halo[face] = jnp.zeros(v_halo.shape[1:], jnp.float32)

    for x in range(cx):
        eps[x] = permit(c[x], permittivity)
    total[...] = jnp.zeros_like(total)
    left_1[...] = jnp.zeros_like(left_1)
    right_1[...] = jnp.zeros_like(right_1)

    z_at = lax.broadcasted_iota(jnp.int32, (cz, ny), 0)
    y_at = lax.broadcasted_iota(jnp.int32, (cz, ny), 1)

    def plane(x, low_x, left, right):
        after = jnp.minimum(x + 1, cx - 1)
        before = jnp.maximum(x - 1, 0)
        own = eps[x]
        high_x = harmonic(own, eps[after]) * jnp.where(x < cx - 1, 1.0, 0.0)
        high_z = jnp.where(z_at < cz - 1, harmonic(own, pltpu.roll(own, cz - 1, 0)), 0.0)
        high_y = jnp.where(y_at < ny - 1, harmonic(own, pltpu.roll(own, ny - 1, 1)), 0.0)
        for k in range(count):
            value = v[k, x]
            flow_z = high_z * (value - pltpu.roll(value, cz - 1, 0))
            flow_y = high_y * (value - pltpu.roll(value, ny - 1, 1))
            result = high_x * (value - v[k, after]) + low_x * (value - v[k, before])
            result = result + (flow_z - pltpu.roll(flow_z, 1, 0))
            result = result + (flow_y - pltpu.roll(flow_y, 1, 1))
            applied[k, x] = result
            store_split(left, k * cz, value)
            store_split(right, k * cz, result)
        return high_x

    def pair(index, low_x):
        low_x = plane(2 * index, low_x, left_0, right_0)
        total[...] += contract(left_1[...], right_1[...])
        low_x = plane(2 * index + 1, low_x, left_1, right_1)
        total[...] += contract(left_0[...], right_0[...])
        return low_x

    lax.fori_loop(0, cx // 2, pair, jnp.zeros((cz, ny), jnp.float32))
    total[...] += contract(left_1[...], right_1[...])

    size = count * cz
    s = a * nz + b
    offsets = (0, -nz, nz, -1, 1)
    row = lax.broadcasted_iota(jnp.int32, (size, nz * width), 0) // cz
    column = lax.broadcasted_iota(jnp.int32, (size, nz * width), 1)
    inside = column % width
    target = (column // width) * (nx * count) + inside
    for j in range(5):
        hit = (target == (s + offsets[j]) * count + row) & (inside < nx * count)
        select[j * size:(j + 1) * size] = jnp.where(hit, 1.0, 0.0).astype(jnp.bfloat16)

    own_block = fold(total[...])
    for face in range(4):
        @pl.when(present[face])
        def _():
            arrival(face, c_source[face], c_halo, c_send, c_recv).wait_recv()
        end = ends[face]
        inner = eps[end] if face < 2 else eps[:, end, :]
        weight = harmonic(inner, permit(c_halo[face], permittivity))
        weight = weight * jnp.where(present[face], 1.0, 0.0)
        for k in range(count):
            value = v[k, end] if face < 2 else v_face[face - 2, k]
            weighted = weight * value
            store_split(left_0 if face % 2 == 0 else left_1, k * cz, weighted)
            store_split(right_0, k * cz, value)
            if face < 2:
                applied[k, end] += weighted
            else:
                applied[k, :, end, :] += weighted
        left = left_0 if face % 2 == 0 else left_1
        own_block = own_block + fold(contract(left[...], right_0[...]))

        @pl.when(present[face])
        def _():
            arrival(face, v_source[face], v_halo, v_send, v_recv).wait_recv()
        for k in range(count):
            store_split(right_1, k * cz, v_halo[face, k])
        blocks[:, (face + 1) * size:(face + 2) * size] = -fold(contract(left[...], right_1[...]))
    blocks[:, :size] = own_block

    same = (
        lax.broadcasted_iota(jnp.int32, blocks.shape, 0) % cz
        == lax.broadcasted_iota(jnp.int32, blocks.shape, 1) % cz
    )
    kept = jnp.where(same, blocks[...], 0.0).reshape(count, cz, blocks.shape[1])
    kept = jnp.sum(kept, axis=1) * (1.0 / (cz * ny))
    high = kept.astype(jnp.bfloat16)
    rest = kept - high.astype(jnp.float32)
    middle = rest.astype(jnp.bfloat16)
    low = (rest - middle.astype(jnp.float32)).astype(jnp.bfloat16)
    placed = sum(
        jnp.dot(part, select[...], preferred_element_type=jnp.float32)
        for part in (low, middle, high)
    )
    for tile in range(nz):
        strip[tile] = placed[:, tile * width:(tile + 1) * width]

    def send_strip(step):
        peer = lax.rem(b + step, nz)
        return pltpu.make_async_remote_copy(
            src_ref=strip.at[peer], dst_ref=rows.at[b], send_sem=strip_send.at[step],
            recv_sem=strip_recv.at[step], device_id=(a, peer), device_id_type=MESH,
        )

    for step in range(1, nz):
        send_strip(step).start()
    rows[b] = strip[b]
    for face in range(4):
        @pl.when(present[face])
        def _():
            copies(face, c_source[face], c_halo, c_send, c_recv).wait_send()
            copies(face, v_source[face], v_halo, v_send, v_recv).wait_send()
    for step in range(1, nz):
        send_strip(step).wait()
    for tile in range(nz):
        coarse[tile * count:(tile + 1) * count, :] = rows[tile, :, :nx * count]


def shards(nx, nz, vectors, classes, permittivity):
    count, cx, cz, ny = vectors.shape
    width = -(-nx * count // LANES) * LANES
    size = count * cz
    f32, i32, bf16 = jnp.float32, jnp.int32, jnp.bfloat16
    dma = pltpu.SemaphoreType.DMA
    return pl.pallas_call(
        functools.partial(kernel, nx, nz),
        out_shape=(
            jax.ShapeDtypeStruct(vectors.shape, f32),
            jax.ShapeDtypeStruct((nz * count, nx * count), f32),
        ),
        in_specs=[
            pl.BlockSpec(memory_space=pl.ANY),
            pl.BlockSpec(memory_space=pl.ANY),
            pl.BlockSpec(memory_space=pltpu.SMEM),
        ],
        out_specs=(
            pl.BlockSpec(memory_space=pltpu.VMEM),
            pl.BlockSpec(memory_space=pltpu.VMEM),
        ),
        scratch_shapes=[
            pltpu.VMEM(vectors.shape, f32),
            pltpu.VMEM(classes.shape, i32),
            pltpu.VMEM(classes.shape, f32),
            pltpu.VMEM((2, cx, ny), i32),
            pltpu.VMEM((2, count, cx, ny), f32),
            pltpu.VMEM((4, cz, ny), i32),
            pltpu.VMEM((4, count, cz, ny), f32),
            pltpu.VMEM((2 * size, ny), bf16),
            pltpu.VMEM((2 * size, ny), bf16),
            pltpu.VMEM((2 * size, ny), bf16),
            pltpu.VMEM((2 * size, ny), bf16),
            pltpu.VMEM((2 * size, 2 * size), f32),
            pltpu.VMEM((size, 5 * size), f32),
            pltpu.VMEM((5 * size, nz * width), bf16),
            pltpu.VMEM((nz, count, width), f32),
            pltpu.VMEM((nz, count, width), f32),
            dma((2,)), dma((4,)), dma((4,)), dma((4,)), dma((4,)), dma((nz,)), dma((nz,)),
        ],
        compiler_params=pltpu.CompilerParams(
            collective_id=0, has_side_effects=True, vmem_limit_bytes=56 * 2**20
        ),
        cost_estimate=pl.CostEstimate(
            flops=2 * 4 * size * size * cx * ny, bytes_accessed=9 * 2**20, transcendentals=0
        ),
    )(vectors, classes, permittivity)


def solution(mesh):
    return jax.shard_map(
        functools.partial(shards, mesh.shape["gx"], mesh.shape["yz"]),
        mesh=mesh,
        in_specs=(P(None, "gx", "yz", None), P("gx", "yz", None), P()),
        out_specs=(P(None, "gx", "yz", None), P("gx", "yz")),
        check_vma=False,
    )
```

```python
import functools

import jax
import jax.numpy as jnp
from jax import lax
from jax.experimental import pallas as pl
from jax.experimental.pallas import tpu as pltpu
from jax.sharding import PartitionSpec as P

MESH = pl.DeviceIdType.MESH
LANES = 128


def permit(classes, permittivity):
    value = jnp.full(classes.shape, permittivity[0], jnp.float32)
    for index in range(1, permittivity.shape[0]):
        value = jnp.where(classes == index, permittivity[index], value)
    return value


def harmonic(first_value, second_value):
    return 2.0 * first_value * second_value / (first_value + second_value)


def split(value):
    high = value.astype(jnp.bfloat16)
    return high, (value - high.astype(jnp.float32)).astype(jnp.bfloat16)


def contract(left, right):
    return lax.dot_general(
        left, right, (((1,), (1,)), ((), ())), preferred_element_type=jnp.float32
    )


def store_split(target, row, value):
    rows = target.shape[0] // 2
    size = value.shape[0]
    high, low = split(value)
    target[row:row + size] = high
    target[rows + row:rows + row + size] = low


def fold(product):
    rows, columns = product.shape[0] // 2, product.shape[1] // 2
    return (
        product[:rows, :columns]
        + product[:rows, columns:]
        + product[rows:, :columns]
        + product[rows:, columns:]
    )


def kernel(
    nx, nz, v_hbm, c_hbm, permittivity, applied, coarse,
    v, c, eps, c_face, v_face, c_halo, v_halo,
    left_0, right_0, left_1, right_1, total, blocks, select, strip, rows,
    face_sem, load_sem, c_send, c_recv, v_send, v_recv, strip_send, strip_recv,
):
    a, b = lax.axis_index("gx"), lax.axis_index("yz")
    count, cx, cz, ny = v.shape
    width = strip.shape[2]
    neighbour = ((a - 1, b), (a + 1, b), (a, b - 1), (a, b + 1))
    present = (a > 0, a < nx - 1, b > 0, b < nz - 1)

    def load(index):
        part = pl.ds(2 * index, 2)
        return pltpu.make_async_copy(v_hbm.at[:, part], v.at[:, part], load_sem.at[index])

    load_c = pltpu.make_async_copy(c_hbm, c, face_sem.at[0])
    load_low = pltpu.make_async_copy(v_hbm.at[:, :, 0, :], v_face.at[0], face_sem.at[1])
    load_high = pltpu.make_async_copy(v_hbm.at[:, :, cz - 1, :], v_face.at[1], face_sem.at[2])
    load_c.start()
    load_low.start()
    load_high.start()
    for index in range(cx // 2):
        load(index).start()

    barrier = pltpu.get_barrier_semaphore()
    for face in range(2):
        @pl.when(present[face])
        def _():
            pl.semaphore_signal(barrier, inc=1, device_id=neighbour[face], device_id_type=MESH)
    for step in range(1, nz):
        pl.semaphore_signal(
            barrier, inc=1, device_id=(a, lax.rem(b + step, nz)), device_id_type=MESH
        )
    partners = (a > 0).astype(jnp.int32) + (a < nx - 1).astype(jnp.int32) + (nz - 1)

    def copies(face, source, halo, send, recv):
        return pltpu.make_async_remote_copy(
            src_ref=source, dst_ref=halo.at[face ^ 1], send_sem=send.at[face],
            recv_sem=recv.at[face ^ 1], device_id=neighbour[face], device_id_type=MESH,
        )

    def arrival(face, source, halo, send, recv):
        return pltpu.make_async_remote_copy(
            src_ref=source, dst_ref=halo.at[face], send_sem=send.at[face],
            recv_sem=recv.at[face], device_id=neighbour[face], device_id_type=MESH,
        )

    ends = (0, cx - 1, 0, cz - 1)
    c_source = tuple(c_hbm.at[ends[f]] if f < 2 else c_face.at[f - 2] for f in range(4))
    v_source = tuple(v_hbm.at[:, ends[f]] if f < 2 else v_face.at[f - 2] for f in range(4))

    load_c.wait()
    for face in (2, 3):
        c_face[face - 2] = c[:, ends[face], :]
    load_low.wait()
    load_high.wait()
    pl.semaphore_wait(barrier, partners)
    for face in (2, 3, 0, 1):
        @pl.when(present[face])
        def _():
            copies(face, c_source[face], c_halo, c_send, c_recv).start()
    for face in (2, 3, 0, 1):
        @pl.when(present[face])
        def _():
            copies(face, v_source[face], v_halo, v_send, v_recv).start()

    for face in range(4):
        @pl.when(jnp.logical_not(present[face]))
        def _():
            c_halo[face] = jnp.zeros(c_halo.shape[1:], jnp.int32)
            v_halo[face] = jnp.zeros(v_halo.shape[1:], jnp.float32)

    for x in range(cx):
        eps[x] = permit(c[x], permittivity)
    total[...] = jnp.zeros_like(total)
    left_1[...] = jnp.zeros_like(left_1)
    right_1[...] = jnp.zeros_like(right_1)

    z_at = lax.broadcasted_iota(jnp.int32, (cz, ny), 0)
    y_at = lax.broadcasted_iota(jnp.int32, (cz, ny), 1)

    def plane(x, low_x, left, right):
        after = jnp.minimum(x + 1, cx - 1)
        before = jnp.maximum(x - 1, 0)
        own = eps[x]
        high_x = harmonic(own, eps[after]) * jnp.where(x < cx - 1, 1.0, 0.0)
        high_z = jnp.where(z_at < cz - 1, harmonic(own, pltpu.roll(own, cz - 1, 0)), 0.0)
        high_y = jnp.where(y_at < ny - 1, harmonic(own, pltpu.roll(own, ny - 1, 1)), 0.0)
        for k in range(count):
            value = v[k, x]
            flow_z = high_z * (value - pltpu.roll(value, cz - 1, 0))
            flow_y = high_y * (value - pltpu.roll(value, ny - 1, 1))
            result = high_x * (value - v[k, after]) + low_x * (value - v[k, before])
            result = result + (flow_z - pltpu.roll(flow_z, 1, 0))
            result = result + (flow_y - pltpu.roll(flow_y, 1, 1))
            applied[k, x] = result
            store_split(left, k * cz, value)
            store_split(right, k * cz, result)
        return high_x

    def pair(index, low_x):
        @pl.when(index < cx // 2 - 1)
        def _():
            load(index + 1).wait()
        low_x = plane(2 * index, low_x, left_0, right_0)
        total[...] += contract(left_1[...], right_1[...])
        low_x = plane(2 * index + 1, low_x, left_1, right_1)
        total[...] += contract(left_0[...], right_0[...])
        return low_x

    load(0).wait()
    lax.fori_loop(0, cx // 2, pair, jnp.zeros((cz, ny), jnp.float32))
    total[...] += contract(left_1[...], right_1[...])

    size = count * cz
    s = a * nz + b
    offsets = (0, -nz, nz, -1, 1)
    row = lax.broadcasted_iota(jnp.int32, (size, nz * width), 0) // cz
    column = lax.broadcasted_iota(jnp.int32, (size, nz * width), 1)
    inside = column % width
    target = (column // width) * (nx * count) + inside
    for j in range(5):
        hit = (target == (s + offsets[j]) * count + row) & (inside < nx * count)
        select[j * size:(j + 1) * size] = jnp.where(hit, 1.0, 0.0).astype(jnp.bfloat16)

    own_block = fold(total[...])
    for face in range(4):
        @pl.when(present[face])
        def _():
            arrival(face, c_source[face], c_halo, c_send, c_recv).wait_recv()
        end = ends[face]
        inner = eps[end] if face < 2 else eps[:, end, :]
        weight = harmonic(inner, permit(c_halo[face], permittivity))
        weight = weight * jnp.where(present[face], 1.0, 0.0)
        for k in range(count):
            value = v[k, end] if face < 2 else v_face[face - 2, k]
            weighted = weight * value
            store_split(left_0 if face % 2 == 0 else left_1, k * cz, weighted)
            store_split(right_0, k * cz, value)
            if face < 2:
                applied[k, end] += weighted
            else:
                applied[k, :, end, :] += weighted
        left = left_0 if face % 2 == 0 else left_1
        own_block = own_block + fold(contract(left[...], right_0[...]))

        @pl.when(present[face])
        def _():
            arrival(face, v_source[face], v_halo, v_send, v_recv).wait_recv()
        for k in range(count):
            store_split(right_1, k * cz, v_halo[face, k])
        blocks[:, (face + 1) * size:(face + 2) * size] = -fold(contract(left[...], right_1[...]))
    blocks[:, :size] = own_block

    same = (
        lax.broadcasted_iota(jnp.int32, blocks.shape, 0) % cz
        == lax.broadcasted_iota(jnp.int32, blocks.shape, 1) % cz
    )
    kept = jnp.where(same, blocks[...], 0.0).reshape(count, cz, blocks.shape[1])
    kept = jnp.sum(kept, axis=1) * (1.0 / (cz * ny))
    high = kept.astype(jnp.bfloat16)
    rest = kept - high.astype(jnp.float32)
    middle = rest.astype(jnp.bfloat16)
    low = (rest - middle.astype(jnp.float32)).astype(jnp.bfloat16)
    placed = sum(
        jnp.dot(part, select[...], preferred_element_type=jnp.float32)
        for part in (low, middle, high)
    )
    for tile in range(nz):
        strip[tile] = placed[:, tile * width:(tile + 1) * width]

    def send_strip(step):
        peer = lax.rem(b + step, nz)
        return pltpu.make_async_remote_copy(
            src_ref=strip.at[peer], dst_ref=rows.at[b], send_sem=strip_send.at[step],
            recv_sem=strip_recv.at[step], device_id=(a, peer), device_id_type=MESH,
        )

    for step in range(1, nz):
        send_strip(step).start()
    rows[b] = strip[b]
    for face in range(4):
        @pl.when(present[face])
        def _():
            copies(face, c_source[face], c_halo, c_send, c_recv).wait_send()
            copies(face, v_source[face], v_halo, v_send, v_recv).wait_send()
    for step in range(1, nz):
        send_strip(step).wait()
    for tile in range(nz):
        coarse[tile * count:(tile + 1) * count, :] = rows[tile, :, :nx * count]


def store(applied, coarse, applied_out, coarse_out, sem):
    copies = (
        pltpu.make_async_copy(applied, applied_out, sem.at[0]),
        pltpu.make_async_copy(coarse, coarse_out, sem.at[1]),
    )
    for copy in copies:
        copy.start()
    for copy in copies:
        copy.wait()


def shards(nx, nz, vectors, classes, permittivity):
    count, cx, cz, ny = vectors.shape
    width = -(-nx * count // LANES) * LANES
    size = count * cz
    f32, i32, bf16 = jnp.float32, jnp.int32, jnp.bfloat16
    dma = pltpu.SemaphoreType.DMA
    results = pl.pallas_call(
        functools.partial(kernel, nx, nz),
        out_shape=(
            jax.ShapeDtypeStruct(vectors.shape, f32),
            jax.ShapeDtypeStruct((nz * count, nx * count), f32),
        ),
        in_specs=[
            pl.BlockSpec(memory_space=pltpu.HBM),
            pl.BlockSpec(memory_space=pltpu.HBM),
            pl.BlockSpec(memory_space=pltpu.SMEM),
        ],
        out_specs=(
            pl.BlockSpec(memory_space=pltpu.VMEM),
            pl.BlockSpec(memory_space=pltpu.VMEM),
        ),
        scratch_shapes=[
            pltpu.VMEM(vectors.shape, f32),
            pltpu.VMEM(classes.shape, i32),
            pltpu.VMEM(classes.shape, f32),
            pltpu.VMEM((2, cx, ny), i32),
            pltpu.VMEM((2, count, cx, ny), f32),
            pltpu.VMEM((4, cz, ny), i32),
            pltpu.VMEM((4, count, cz, ny), f32),
            pltpu.VMEM((2 * size, ny), bf16),
            pltpu.VMEM((2 * size, ny), bf16),
            pltpu.VMEM((2 * size, ny), bf16),
            pltpu.VMEM((2 * size, ny), bf16),
            pltpu.VMEM((2 * size, 2 * size), f32),
            pltpu.VMEM((size, 5 * size), f32),
            pltpu.VMEM((5 * size, nz * width), bf16),
            pltpu.VMEM((nz, count, width), f32),
            pltpu.VMEM((nz, count, width), f32),
            dma((3,)), dma((cx // 2,)), dma((4,)), dma((4,)), dma((4,)), dma((4,)), dma((nz,)), dma((nz,)),
        ],
        compiler_params=pltpu.CompilerParams(
            collective_id=0, has_side_effects=True, vmem_limit_bytes=48 * 2**20
        ),
        cost_estimate=pl.CostEstimate(
            flops=2 * 4 * size * size * cx * ny, bytes_accessed=9 * 2**20, transcendentals=0
        ),
    )(vectors, classes, permittivity)
    return pl.pallas_call(
        store,
        out_shape=tuple(jax.ShapeDtypeStruct(result.shape, f32) for result in results),
        in_specs=[pl.BlockSpec(memory_space=pl.ANY)] * 2,
        out_specs=(pl.BlockSpec(memory_space=pltpu.HBM),) * 2,
        scratch_shapes=[dma((2,))],
        cost_estimate=pl.CostEstimate(flops=0, bytes_accessed=8 * 2**20, transcendentals=0),
    )(*results)


def solution(mesh):
    return jax.shard_map(
        functools.partial(shards, mesh.shape["gx"], mesh.shape["yz"]),
        mesh=mesh,
        in_specs=(P(None, "gx", "yz", None), P("gx", "yz", None), P()),
        out_specs=(P(None, "gx", "yz", None), P("gx", "yz")),
        check_vma=False,
    )
```

```python
import functools

import jax
import jax.numpy as jnp
from jax import lax
from jax.experimental import pallas as pl
from jax.experimental.pallas import tpu as pltpu
from jax.sharding import PartitionSpec as P

MESH = pl.DeviceIdType.MESH
LANES = 128


def permit(classes, permittivity):
    value = jnp.full(classes.shape, permittivity[0], jnp.float32)
    for index in range(1, permittivity.shape[0]):
        value = jnp.where(classes == index, permittivity[index], value)
    return value


def harmonic(first_value, second_value):
    return 2.0 * first_value * second_value / (first_value + second_value)


def split(value):
    high = value.astype(jnp.bfloat16)
    return high, (value - high.astype(jnp.float32)).astype(jnp.bfloat16)


def contract(left, right):
    return lax.dot_general(
        left, right, (((1,), (1,)), ((), ())), preferred_element_type=jnp.float32
    )


def store_split(target, row, value, face=0):
    rows = target.shape[0] // 2
    size, columns = value.shape
    high, low = split(value)
    lanes = slice(face * columns, (face + 1) * columns)
    target[row:row + size, lanes] = high
    target[rows + row:rows + row + size, lanes] = low


def fold(product):
    rows, columns = product.shape[0] // 2, product.shape[1] // 2
    return (
        product[:rows, :columns]
        + product[:rows, columns:]
        + product[rows:, :columns]
        + product[rows:, columns:]
    )


def kernel(
    nx, nz, v_hbm, c_hbm, permittivity, applied, coarse,
    v, c, eps, c_face, v_face, c_halo, v_halo,
    left_0, right_0, left_1, right_1, flow_x, left_f, own_f, halo_f, total, blocks, select, strip, rows,
    face_sem, load_sem, c_send, c_recv, v_send, v_recv, strip_send, strip_recv,
):
    a, b = lax.axis_index("gx"), lax.axis_index("yz")
    count, cx, cz, ny = v.shape
    width = strip.shape[2]
    neighbour = ((a - 1, b), (a + 1, b), (a, b - 1), (a, b + 1))
    present = (a > 0, a < nx - 1, b > 0, b < nz - 1)

    def load(index):
        part = pl.ds(2 * index, 2)
        return pltpu.make_async_copy(v_hbm.at[:, part], v.at[:, part], load_sem.at[index])

    load_c = pltpu.make_async_copy(c_hbm, c, face_sem.at[0])
    load_low = pltpu.make_async_copy(v_hbm.at[:, :, 0, :], v_face.at[0], face_sem.at[1])
    load_high = pltpu.make_async_copy(v_hbm.at[:, :, cz - 1, :], v_face.at[1], face_sem.at[2])
    load_c.start()
    load_low.start()
    load_high.start()
    for index in range(cx // 2):
        load(index).start()

    barrier = pltpu.get_barrier_semaphore()
    for face in range(2):
        @pl.when(present[face])
        def _():
            pl.semaphore_signal(barrier, inc=1, device_id=neighbour[face], device_id_type=MESH)
    for step in range(1, nz):
        pl.semaphore_signal(
            barrier, inc=1, device_id=(a, lax.rem(b + step, nz)), device_id_type=MESH
        )
    partners = (a > 0).astype(jnp.int32) + (a < nx - 1).astype(jnp.int32) + (nz - 1)

    def copies(face, source, halo, send, recv):
        return pltpu.make_async_remote_copy(
            src_ref=source, dst_ref=halo.at[face ^ 1], send_sem=send.at[face],
            recv_sem=recv.at[face ^ 1], device_id=neighbour[face], device_id_type=MESH,
        )

    def arrival(face, source, halo, send, recv):
        return pltpu.make_async_remote_copy(
            src_ref=source, dst_ref=halo.at[face], send_sem=send.at[face],
            recv_sem=recv.at[face], device_id=neighbour[face], device_id_type=MESH,
        )

    ends = (0, cx - 1, 0, cz - 1)
    c_source = tuple(c_hbm.at[ends[f]] if f < 2 else c_face.at[f - 2] for f in range(4))
    v_source = tuple(v_hbm.at[:, ends[f]] if f < 2 else v_face.at[f - 2] for f in range(4))

    load_c.wait()
    for face in (2, 3):
        c_face[face - 2] = c[:, ends[face], :]
    load_low.wait()
    load_high.wait()
    pl.semaphore_wait(barrier, partners)
    for face in (2, 3, 0, 1):
        @pl.when(present[face])
        def _():
            copies(face, c_source[face], c_halo, c_send, c_recv).start()
    for face in (2, 3, 0, 1):
        @pl.when(present[face])
        def _():
            copies(face, v_source[face], v_halo, v_send, v_recv).start()

    for face in range(4):
        @pl.when(jnp.logical_not(present[face]))
        def _():
            c_halo[face] = jnp.zeros(c_halo.shape[1:], jnp.int32)
            v_halo[face] = jnp.zeros(v_halo.shape[1:], jnp.float32)

    for x in range(cx):
        eps[x] = permit(c[x], permittivity)
    total[...] = jnp.zeros_like(total)
    left_1[...] = jnp.zeros_like(left_1)
    right_1[...] = jnp.zeros_like(right_1)

    z_at = lax.broadcasted_iota(jnp.int32, (cz, ny), 0)
    y_at = lax.broadcasted_iota(jnp.int32, (cz, ny), 1)

    flow_x[...] = jnp.zeros_like(flow_x)

    def plane(x, left, right):
        after = jnp.minimum(x + 1, cx - 1)
        own = eps[x]
        high_x = harmonic(own, eps[after]) * jnp.where(x < cx - 1, 1.0, 0.0)
        high_z = jnp.where(z_at < cz - 1, harmonic(own, pltpu.roll(own, cz - 1, 0)), 0.0)
        high_y = jnp.where(y_at < ny - 1, harmonic(own, pltpu.roll(own, ny - 1, 1)), 0.0)
        for k in range(count):
            value = v[k, x]
            flow_z = high_z * (value - pltpu.roll(value, cz - 1, 0))
            flow_y = high_y * (value - pltpu.roll(value, ny - 1, 1))
            flow = high_x * (value - v[k, after])
            result = flow - flow_x[k]
            flow_x[k] = flow
            result = result + (flow_z - pltpu.roll(flow_z, 1, 0))
            result = result + (flow_y - pltpu.roll(flow_y, 1, 1))
            applied[k, x] = result
            store_split(left, k * cz, value)
            store_split(right, k * cz, result)

    def pair(index, carry):
        @pl.when(index < cx // 2 - 1)
        def _():
            load(index + 1).wait()
        plane(2 * index, left_0, right_0)
        total[...] += contract(left_1[...], right_1[...])
        plane(2 * index + 1, left_1, right_1)
        total[...] += contract(left_0[...], right_0[...])
        return carry

    load(0).wait()
    lax.fori_loop(0, cx // 2, pair, 0)
    size = count * cz
    s = a * nz + b
    offsets = (0, -nz, nz, -1, 1)
    row = lax.broadcasted_iota(jnp.int32, (size, nz * width), 0) // cz
    column = lax.broadcasted_iota(jnp.int32, (size, nz * width), 1)
    inside = column % width
    target = (column // width) * (nx * count) + inside
    for j in range(5):
        hit = (target == (s + offsets[j]) * count + row) & (inside < nx * count)
        select[j * size:(j + 1) * size] = jnp.where(hit, 1.0, 0.0).astype(jnp.bfloat16)

    for face in range(4):
        @pl.when(present[face])
        def _():
            arrival(face, c_source[face], c_halo, c_send, c_recv).wait_recv()
    for face in range(4):
        end = ends[face]
        inner = eps[end] if face < 2 else eps[:, end, :]
        weight = harmonic(inner, permit(c_halo[face], permittivity))
        weight = weight * jnp.where(present[face], 1.0, 0.0)
        for k in range(count):
            value = v[k, end] if face < 2 else v_face[face - 2, k]
            weighted = weight * value
            store_split(left_f, k * cz, weighted, face)
            store_split(own_f, k * cz, value, face)
            if face < 2:
                applied[k, end] += weighted
            else:
                applied[k, :, end, :] += weighted
    total[...] += contract(left_1[...], right_1[...])
    own_block = fold(total[...] + contract(left_f[...], own_f[...]))

    for face in range(4):
        @pl.when(present[face])
        def _():
            arrival(face, v_source[face], v_halo, v_send, v_recv).wait_recv()
    for face in range(4):
        lanes = slice(face * ny, (face + 1) * ny)
        for k in range(count):
            store_split(halo_f, k * cz, v_halo[face, k], face)
        blocks[:, (face + 1) * size:(face + 2) * size] = -fold(
            contract(left_f[:, lanes], halo_f[:, lanes])
        )
    blocks[:, :size] = own_block

    same = (
        lax.broadcasted_iota(jnp.int32, blocks.shape, 0) % cz
        == lax.broadcasted_iota(jnp.int32, blocks.shape, 1) % cz
    )
    kept = jnp.where(same, blocks[...], 0.0).reshape(count, cz, blocks.shape[1])
    kept = jnp.sum(kept, axis=1) * (1.0 / (cz * ny))
    high = kept.astype(jnp.bfloat16).astype(jnp.float32)
    rest = kept - high
    middle = rest.astype(jnp.bfloat16).astype(jnp.float32)
    parts = jnp.concatenate([rest - middle, middle, high], axis=0).astype(jnp.bfloat16)
    placed = jnp.dot(parts, select[...], preferred_element_type=jnp.float32)
    placed = placed[:count] + placed[count:2 * count] + placed[2 * count:]
    for tile in range(nz):
        strip[tile] = placed[:, tile * width:(tile + 1) * width]

    def send_strip(step):
        peer = lax.rem(b + step, nz)
        return pltpu.make_async_remote_copy(
            src_ref=strip.at[peer], dst_ref=rows.at[b], send_sem=strip_send.at[step],
            recv_sem=strip_recv.at[step], device_id=(a, peer), device_id_type=MESH,
        )

    for step in range(1, nz):
        send_strip(step).start()
    rows[b] = strip[b]
    for face in range(4):
        @pl.when(present[face])
        def _():
            copies(face, c_source[face], c_halo, c_send, c_recv).wait_send()
            copies(face, v_source[face], v_halo, v_send, v_recv).wait_send()
    for step in range(1, nz):
        send_strip(step).wait()
    for tile in range(nz):
        coarse[tile * count:(tile + 1) * count, :] = rows[tile, :, :nx * count]


def store(applied, coarse, applied_out, coarse_out, sem):
    copies = (
        pltpu.make_async_copy(applied, applied_out, sem.at[0]),
        pltpu.make_async_copy(coarse, coarse_out, sem.at[1]),
    )
    for copy in copies:
        copy.start()
    for copy in copies:
        copy.wait()


def shards(nx, nz, vectors, classes, permittivity):
    count, cx, cz, ny = vectors.shape
    width = -(-nx * count // LANES) * LANES
    size = count * cz
    f32, i32, bf16 = jnp.float32, jnp.int32, jnp.bfloat16
    dma = pltpu.SemaphoreType.DMA
    results = pl.pallas_call(
        functools.partial(kernel, nx, nz),
        out_shape=(
            jax.ShapeDtypeStruct(vectors.shape, f32),
            jax.ShapeDtypeStruct((nz * count, nx * count), f32),
        ),
        in_specs=[
            pl.BlockSpec(memory_space=pltpu.HBM),
            pl.BlockSpec(memory_space=pltpu.HBM),
            pl.BlockSpec(memory_space=pltpu.SMEM),
        ],
        out_specs=(
            pl.BlockSpec(memory_space=pltpu.VMEM),
            pl.BlockSpec(memory_space=pltpu.VMEM),
        ),
        scratch_shapes=[
            pltpu.VMEM(vectors.shape, f32),
            pltpu.VMEM(classes.shape, i32),
            pltpu.VMEM(classes.shape, f32),
            pltpu.VMEM((2, cx, ny), i32),
            pltpu.VMEM((2, count, cx, ny), f32),
            pltpu.VMEM((4, cz, ny), i32),
            pltpu.VMEM((4, count, cz, ny), f32),
            pltpu.VMEM((2 * size, ny), bf16),
            pltpu.VMEM((2 * size, ny), bf16),
            pltpu.VMEM((2 * size, ny), bf16),
            pltpu.VMEM((2 * size, ny), bf16),
            pltpu.VMEM((count, cz, ny), f32),
            pltpu.VMEM((2 * size, 4 * ny), bf16),
            pltpu.VMEM((2 * size, 4 * ny), bf16),
            pltpu.VMEM((2 * size, 4 * ny), bf16),
            pltpu.VMEM((2 * size, 2 * size), f32),
            pltpu.VMEM((size, 5 * size), f32),
            pltpu.VMEM((5 * size, nz * width), bf16),
            pltpu.VMEM((nz, count, width), f32),
            pltpu.VMEM((nz, count, width), f32),
            dma((3,)), dma((cx // 2,)), dma((4,)), dma((4,)), dma((4,)), dma((4,)), dma((nz,)), dma((nz,)),
        ],
        compiler_params=pltpu.CompilerParams(
            collective_id=0, has_side_effects=True, vmem_limit_bytes=48 * 2**20
        ),
        cost_estimate=pl.CostEstimate(
            flops=2 * 4 * size * size * cx * ny, bytes_accessed=9 * 2**20, transcendentals=0
        ),
    )(vectors, classes, permittivity)
    return pl.pallas_call(
        store,
        out_shape=tuple(jax.ShapeDtypeStruct(result.shape, f32) for result in results),
        in_specs=[pl.BlockSpec(memory_space=pltpu.VMEM)] * 2,
        out_specs=(pl.BlockSpec(memory_space=pl.ANY),) * 2,
        scratch_shapes=[dma((2,))],
        cost_estimate=pl.CostEstimate(flops=0, bytes_accessed=8 * 2**20, transcendentals=0),
    )(*results)


def solution(mesh):
    return jax.shard_map(
        functools.partial(shards, mesh.shape["gx"], mesh.shape["yz"]),
        mesh=mesh,
        in_specs=(P(None, "gx", "yz", None), P("gx", "yz", None), P()),
        out_specs=(P(None, "gx", "yz", None), P("gx", "yz")),
        check_vma=False,
    )
```

```python
import functools

import jax
import jax.numpy as jnp
from jax import lax
from jax.experimental import pallas as pl
from jax.experimental.pallas import tpu as pltpu
from jax.sharding import PartitionSpec as P

MESH = pl.DeviceIdType.MESH
LANES = 128


def permit(classes, permittivity):
    value = jnp.full(classes.shape, permittivity[0], jnp.float32)
    for index in range(1, permittivity.shape[0]):
        value = jnp.where(classes == index, permittivity[index], value)
    return value


def harmonic(first_value, second_value):
    return 2.0 * first_value * second_value / (first_value + second_value)


def split(value):
    high = value.astype(jnp.bfloat16)
    return high, (value - high.astype(jnp.float32)).astype(jnp.bfloat16)


def contract(left, right):
    return lax.dot_general(
        left, right, (((1,), (1,)), ((), ())), preferred_element_type=jnp.float32
    )


def store_split(target, row, value, face=0):
    rows = target.shape[0] // 2
    size, columns = value.shape
    high, low = split(value)
    lanes = slice(face * columns, (face + 1) * columns)
    target[row:row + size, lanes] = high
    target[rows + row:rows + row + size, lanes] = low


def fold(product):
    rows, columns = product.shape[0] // 2, product.shape[1] // 2
    return (
        product[:rows, :columns]
        + product[:rows, columns:]
        + product[rows:, :columns]
        + product[rows:, columns:]
    )


def kernel(
    nx, nz, v_hbm, c_hbm, permittivity, applied, coarse,
    v, c, eps, c_face, v_face, c_halo, v_halo,
    left_0, right_0, left_1, right_1, flow_x, left_f, own_f, halo_f, total, blocks, select, strip, rows,
    face_sem, load_sem, c_send, c_recv, v_send, v_recv, strip_send, strip_recv,
):
    a, b = lax.axis_index("gx"), lax.axis_index("yz")
    count, cx, cz, ny = v.shape
    width = strip.shape[2]
    neighbour = ((a - 1, b), (a + 1, b), (a, b - 1), (a, b + 1))
    present = (a > 0, a < nx - 1, b > 0, b < nz - 1)

    def load(index):
        part = pl.ds(2 * index, 2)
        return pltpu.make_async_copy(v_hbm.at[:, part], v.at[:, part], load_sem.at[index])

    load_c = pltpu.make_async_copy(c_hbm, c, face_sem.at[0])
    load_low = pltpu.make_async_copy(v_hbm.at[:, :, 0, :], v_face.at[0], face_sem.at[1])
    load_high = pltpu.make_async_copy(v_hbm.at[:, :, cz - 1, :], v_face.at[1], face_sem.at[2])
    load_c.start()
    load_low.start()
    load_high.start()
    for index in range(cx // 2):
        load(index).start()

    barrier = pltpu.get_barrier_semaphore()
    for face in range(2):
        @pl.when(present[face])
        def _():
            pl.semaphore_signal(barrier, inc=1, device_id=neighbour[face], device_id_type=MESH)
    for step in range(1, nz):
        pl.semaphore_signal(
            barrier, inc=1, device_id=(a, lax.rem(b + step, nz)), device_id_type=MESH
        )
    partners = (a > 0).astype(jnp.int32) + (a < nx - 1).astype(jnp.int32) + (nz - 1)

    def copies(face, source, halo, send, recv):
        return pltpu.make_async_remote_copy(
            src_ref=source, dst_ref=halo.at[face ^ 1], send_sem=send.at[face],
            recv_sem=recv.at[face ^ 1], device_id=neighbour[face], device_id_type=MESH,
        )

    def arrival(face, source, halo, send, recv):
        return pltpu.make_async_remote_copy(
            src_ref=source, dst_ref=halo.at[face], send_sem=send.at[face],
            recv_sem=recv.at[face], device_id=neighbour[face], device_id_type=MESH,
        )

    ends = (0, cx - 1, 0, cz - 1)
    c_source = tuple(c_hbm.at[ends[f]] if f < 2 else c_face.at[f - 2] for f in range(4))
    v_source = tuple(v_hbm.at[:, ends[f]] if f < 2 else v_face.at[f - 2] for f in range(4))

    load_c.wait()
    for face in (2, 3):
        c_face[face - 2] = c[:, ends[face], :]
    load_low.wait()
    load_high.wait()
    pl.semaphore_wait(barrier, partners)
    for face in (2, 3, 0, 1):
        @pl.when(present[face])
        def _():
            copies(face, c_source[face], c_halo, c_send, c_recv).start()
    for face in (2, 3, 0, 1):
        @pl.when(present[face])
        def _():
            copies(face, v_source[face], v_halo, v_send, v_recv).start()

    for face in range(4):
        @pl.when(jnp.logical_not(present[face]))
        def _():
            c_halo[face] = jnp.zeros(c_halo.shape[1:], jnp.int32)
            v_halo[face] = jnp.zeros(v_halo.shape[1:], jnp.float32)

    for x in range(cx):
        eps[x] = permit(c[x], permittivity)
    total[...] = jnp.zeros_like(total)
    left_1[...] = jnp.zeros_like(left_1)
    right_1[...] = jnp.zeros_like(right_1)

    z_at = lax.broadcasted_iota(jnp.int32, (cz, ny), 0)
    y_at = lax.broadcasted_iota(jnp.int32, (cz, ny), 1)

    flow_x[...] = jnp.zeros_like(flow_x)

    def plane(x, left, right):
        after = jnp.minimum(x + 1, cx - 1)
        own = eps[x]
        high_x = harmonic(own, eps[after]) * jnp.where(x < cx - 1, 1.0, 0.0)
        high_z = jnp.where(z_at < cz - 1, harmonic(own, pltpu.roll(own, cz - 1, 0)), 0.0)
        high_y = jnp.where(y_at < ny - 1, harmonic(own, pltpu.roll(own, ny - 1, 1)), 0.0)
        for k in range(count):
            value = v[k, x]
            flow_z = high_z * (value - pltpu.roll(value, cz - 1, 0))
            flow_y = high_y * (value - pltpu.roll(value, ny - 1, 1))
            flow = high_x * (value - v[k, after])
            result = flow - flow_x[k]
            flow_x[k] = flow
            result = result + (flow_z - pltpu.roll(flow_z, 1, 0))
            result = result + (flow_y - pltpu.roll(flow_y, 1, 1))
            applied[k, x] = result
            store_split(left, k * cz, value)
            store_split(right, k * cz, result)

    def pair(index, carry):
        @pl.when(index < cx // 2 - 1)
        def _():
            load(index + 1).wait()
        plane(2 * index, left_0, right_0)
        total[...] += contract(left_1[...], right_1[...])
        plane(2 * index + 1, left_1, right_1)
        total[...] += contract(left_0[...], right_0[...])
        return carry

    load(0).wait()
    lax.fori_loop(0, cx // 2, pair, 0)
    size = count * cz
    s = a * nz + b
    offsets = (0, -nz, nz, -1, 1)
    row = lax.broadcasted_iota(jnp.int32, (size, nz * width), 0) // cz
    column = lax.broadcasted_iota(jnp.int32, (size, nz * width), 1)
    inside = column % width
    target = (column // width) * (nx * count) + inside
    for j in range(5):
        hit = (target == (s + offsets[j]) * count + row) & (inside < nx * count)
        select[j * size:(j + 1) * size] = jnp.where(hit, 1.0, 0.0).astype(jnp.bfloat16)

    for face in range(4):
        @pl.when(present[face])
        def _():
            arrival(face, c_source[face], c_halo, c_send, c_recv).wait_recv()
    for face in range(4):
        end = ends[face]
        inner = eps[end] if face < 2 else eps[:, end, :]
        weight = harmonic(inner, permit(c_halo[face], permittivity))
        weight = weight * jnp.where(present[face], 1.0, 0.0)
        for k in range(count):
            value = v[k, end] if face < 2 else v_face[face - 2, k]
            weighted = weight * value
            store_split(left_f, k * cz, weighted, face)
            store_split(own_f, k * cz, value, face)
            if face < 2:
                applied[k, end] += weighted
            else:
                applied[k, :, end, :] += weighted
    total[...] += contract(left_1[...], right_1[...])
    own_block = fold(total[...] + contract(left_f[...], own_f[...]))

    for face in range(4):
        @pl.when(present[face])
        def _():
            arrival(face, v_source[face], v_halo, v_send, v_recv).wait_recv()
    for face in range(4):
        lanes = slice(face * ny, (face + 1) * ny)
        for k in range(count):
            store_split(halo_f, k * cz, v_halo[face, k], face)
        blocks[:, (face + 1) * size:(face + 2) * size] = -fold(
            contract(left_f[:, lanes], halo_f[:, lanes])
        )
    blocks[:, :size] = own_block

    same = (
        lax.broadcasted_iota(jnp.int32, blocks.shape, 0) % cz
        == lax.broadcasted_iota(jnp.int32, blocks.shape, 1) % cz
    )
    kept = jnp.where(same, blocks[...], 0.0).reshape(count, cz, blocks.shape[1])
    kept = jnp.sum(kept, axis=1) * (1.0 / (cz * ny))
    high = kept.astype(jnp.bfloat16).astype(jnp.float32)
    rest = kept - high
    middle = rest.astype(jnp.bfloat16).astype(jnp.float32)
    parts = jnp.concatenate([rest - middle, middle, high], axis=0).astype(jnp.bfloat16)
    placed = jnp.dot(parts, select[...], preferred_element_type=jnp.float32)
    placed = placed[:count] + placed[count:2 * count] + placed[2 * count:]
    for tile in range(nz):
        strip[tile] = placed[:, tile * width:(tile + 1) * width]

    def send_strip(step):
        peer = lax.rem(b + step, nz)
        return pltpu.make_async_remote_copy(
            src_ref=strip.at[peer], dst_ref=rows.at[b], send_sem=strip_send.at[step],
            recv_sem=strip_recv.at[step], device_id=(a, peer), device_id_type=MESH,
        )

    for step in range(1, nz):
        send_strip(step).start()
    rows[b] = strip[b]
    for face in range(4):
        @pl.when(present[face])
        def _():
            copies(face, c_source[face], c_halo, c_send, c_recv).wait_send()
            copies(face, v_source[face], v_halo, v_send, v_recv).wait_send()
    for step in range(1, nz):
        send_strip(step).wait()
    for tile in range(nz):
        coarse[tile * count:(tile + 1) * count, :] = rows[tile, :, :nx * count]


def shards(nx, nz, vectors, classes, permittivity):
    count, cx, cz, ny = vectors.shape
    width = -(-nx * count // LANES) * LANES
    size = count * cz
    f32, i32, bf16 = jnp.float32, jnp.int32, jnp.bfloat16
    dma = pltpu.SemaphoreType.DMA
    vectors, classes, permittivity = (
        pltpu.with_memory_space_constraint(array, pltpu.HBM)
        for array in (vectors, classes, permittivity)
    )
    return pl.pallas_call(
        functools.partial(kernel, nx, nz),
        out_shape=(
            jax.ShapeDtypeStruct(vectors.shape, f32),
            jax.ShapeDtypeStruct((nz * count, nx * count), f32),
        ),
        in_specs=[
            pl.BlockSpec(memory_space=pltpu.HBM),
            pl.BlockSpec(memory_space=pltpu.HBM),
            pl.BlockSpec(memory_space=pltpu.SMEM),
        ],
        out_specs=(
            pl.BlockSpec(memory_space=pltpu.VMEM),
            pl.BlockSpec(memory_space=pltpu.VMEM),
        ),
        scratch_shapes=[
            pltpu.VMEM(vectors.shape, f32),
            pltpu.VMEM(classes.shape, i32),
            pltpu.VMEM(classes.shape, f32),
            pltpu.VMEM((2, cx, ny), i32),
            pltpu.VMEM((2, count, cx, ny), f32),
            pltpu.VMEM((4, cz, ny), i32),
            pltpu.VMEM((4, count, cz, ny), f32),
            pltpu.VMEM((2 * size, ny), bf16),
            pltpu.VMEM((2 * size, ny), bf16),
            pltpu.VMEM((2 * size, ny), bf16),
            pltpu.VMEM((2 * size, ny), bf16),
            pltpu.VMEM((count, cz, ny), f32),
            pltpu.VMEM((2 * size, 4 * ny), bf16),
            pltpu.VMEM((2 * size, 4 * ny), bf16),
            pltpu.VMEM((2 * size, 4 * ny), bf16),
            pltpu.VMEM((2 * size, 2 * size), f32),
            pltpu.VMEM((size, 5 * size), f32),
            pltpu.VMEM((5 * size, nz * width), bf16),
            pltpu.VMEM((nz, count, width), f32),
            pltpu.VMEM((nz, count, width), f32),
            dma((3,)), dma((cx // 2,)), dma((4,)), dma((4,)), dma((4,)), dma((4,)), dma((nz,)), dma((nz,)),
        ],
        compiler_params=pltpu.CompilerParams(
            collective_id=0, has_side_effects=True, vmem_limit_bytes=48 * 2**20
        ),
        cost_estimate=pl.CostEstimate(
            flops=2 * 4 * size * size * cx * ny, bytes_accessed=9 * 2**20, transcendentals=0
        ),
    )(vectors, classes, permittivity)


def solution(mesh):
    return jax.shard_map(
        functools.partial(shards, mesh.shape["gx"], mesh.shape["yz"]),
        mesh=mesh,
        in_specs=(P(None, "gx", "yz", None), P("gx", "yz", None), P()),
        out_specs=(P(None, "gx", "yz", None), P("gx", "yz")),
        check_vma=False,
    )
```

```python
import functools

import jax
import jax.numpy as jnp
from jax import lax
from jax.experimental import pallas as pl
from jax.experimental.pallas import tpu as pltpu
from jax.sharding import PartitionSpec as P

MESH = pl.DeviceIdType.MESH
LANES = 128


def permit(classes, permittivity):
    value = jnp.full(classes.shape, permittivity[0], jnp.float32)
    for index in range(1, permittivity.shape[0]):
        value = jnp.where(classes == index, permittivity[index], value)
    return value


def harmonic(first_value, second_value):
    return 2.0 * first_value * second_value / (first_value + second_value)


def split(value):
    high = value.astype(jnp.bfloat16)
    return high, (value - high.astype(jnp.float32)).astype(jnp.bfloat16)


def contract(left, right):
    return lax.dot_general(
        left, right, (((1,), (1,)), ((), ())), preferred_element_type=jnp.float32
    )


def store_split(target, row, value, face=0):
    rows = target.shape[0] // 2
    size, columns = value.shape
    high, low = split(value)
    lanes = slice(face * columns, (face + 1) * columns)
    target[row:row + size, lanes] = high
    target[rows + row:rows + row + size, lanes] = low


def fold(product):
    rows, columns = product.shape[0] // 2, product.shape[1] // 2
    return (
        product[:rows, :columns]
        + product[:rows, columns:]
        + product[rows:, :columns]
        + product[rows:, columns:]
    )


def kernel(
    nx, nz, v_hbm, c_hbm, permittivity, applied, coarse,
    v, c, eps, c_face, v_face, c_halo, v_halo,
    left_0, right_0, left_1, right_1, flow_x, left_f, own_f, halo_f, total, blocks, select, strip, rows,
    face_sem, load_sem, c_send, c_recv, v_send, v_recv, strip_send, strip_recv,
):
    a, b = lax.axis_index("gx"), lax.axis_index("yz")
    count, cx, cz, ny = v.shape
    width = strip.shape[2]
    neighbour = ((a - 1, b), (a + 1, b), (a, b - 1), (a, b + 1))
    present = (a > 0, a < nx - 1, b > 0, b < nz - 1)

    def load(index):
        part = pl.ds(2 * index, 2)
        return pltpu.make_async_copy(v_hbm.at[:, part], v.at[:, part], load_sem.at[index])

    load_c = pltpu.make_async_copy(c_hbm, c, face_sem.at[0])
    load_low = pltpu.make_async_copy(v_hbm.at[:, :, 0, :], v_face.at[0], face_sem.at[1])
    load_high = pltpu.make_async_copy(v_hbm.at[:, :, cz - 1, :], v_face.at[1], face_sem.at[2])
    load_c.start()
    load_low.start()
    load_high.start()
    for index in range(cx // 2):
        load(index).start()

    barrier = pltpu.get_barrier_semaphore()
    for face in range(2):
        @pl.when(present[face])
        def _():
            pl.semaphore_signal(barrier, inc=1, device_id=neighbour[face], device_id_type=MESH)
    for step in range(1, nz):
        pl.semaphore_signal(
            barrier, inc=1, device_id=(a, lax.rem(b + step, nz)), device_id_type=MESH
        )
    partners = (a > 0).astype(jnp.int32) + (a < nx - 1).astype(jnp.int32) + (nz - 1)

    def copies(face, source, halo, send, recv):
        return pltpu.make_async_remote_copy(
            src_ref=source, dst_ref=halo.at[face ^ 1], send_sem=send.at[face],
            recv_sem=recv.at[face ^ 1], device_id=neighbour[face], device_id_type=MESH,
        )

    def arrival(face, source, halo, send, recv):
        return pltpu.make_async_remote_copy(
            src_ref=source, dst_ref=halo.at[face], send_sem=send.at[face],
            recv_sem=recv.at[face], device_id=neighbour[face], device_id_type=MESH,
        )

    ends = (0, cx - 1, 0, cz - 1)
    c_source = tuple(c_hbm.at[ends[f]] if f < 2 else c_face.at[f - 2] for f in range(4))
    v_source = tuple(v_hbm.at[:, ends[f]] if f < 2 else v_face.at[f - 2] for f in range(4))

    size = count * cz
    s = a * nz + b
    offsets = (0, -nz, nz, -1, 1)
    row = lax.broadcasted_iota(jnp.int32, (size, nz * width), 0) // cz
    column = lax.broadcasted_iota(jnp.int32, (size, nz * width), 1)
    inside = column % width
    target = (column // width) * (nx * count) + inside
    for j in range(5):
        hit = (target == (s + offsets[j]) * count + row) & (inside < nx * count)
        select[j * size:(j + 1) * size] = jnp.where(hit, 1.0, 0.0).astype(jnp.bfloat16)
    total[...] = jnp.zeros_like(total)
    left_1[...] = jnp.zeros_like(left_1)
    right_1[...] = jnp.zeros_like(right_1)
    flow_x[...] = jnp.zeros_like(flow_x)

    load_c.wait()
    for face in (2, 3):
        c_face[face - 2] = c[:, ends[face], :]
    for x in range(cx):
        eps[x] = permit(c[x], permittivity)
    load_low.wait()
    load_high.wait()
    pl.semaphore_wait(barrier, partners)
    for face in (2, 3, 0, 1):
        @pl.when(present[face])
        def _():
            copies(face, c_source[face], c_halo, c_send, c_recv).start()
    for face in (2, 3, 0, 1):
        @pl.when(present[face])
        def _():
            copies(face, v_source[face], v_halo, v_send, v_recv).start()

    for face in range(4):
        @pl.when(jnp.logical_not(present[face]))
        def _():
            c_halo[face] = jnp.zeros(c_halo.shape[1:], jnp.int32)
            v_halo[face] = jnp.zeros(v_halo.shape[1:], jnp.float32)

    z_at = lax.broadcasted_iota(jnp.int32, (cz, ny), 0)
    y_at = lax.broadcasted_iota(jnp.int32, (cz, ny), 1)

    def plane(x, left, right):
        after = jnp.minimum(x + 1, cx - 1)
        own = eps[x]
        high_x = harmonic(own, eps[after]) * jnp.where(x < cx - 1, 1.0, 0.0)
        high_z = jnp.where(z_at < cz - 1, harmonic(own, pltpu.roll(own, cz - 1, 0)), 0.0)
        high_y = jnp.where(y_at < ny - 1, harmonic(own, pltpu.roll(own, ny - 1, 1)), 0.0)
        for k in range(count):
            value = v[k, x]
            flow_z = high_z * (value - pltpu.roll(value, cz - 1, 0))
            flow_y = high_y * (value - pltpu.roll(value, ny - 1, 1))
            flow = high_x * (value - v[k, after])
            result = flow - flow_x[k]
            flow_x[k] = flow
            result = result + (flow_z - pltpu.roll(flow_z, 1, 0))
            result = result + (flow_y - pltpu.roll(flow_y, 1, 1))
            applied[k, x] = result
            store_split(left, k * cz, value)
            store_split(right, k * cz, result)

    def pair(index, carry):
        @pl.when(index < cx // 2 - 1)
        def _():
            load(index + 1).wait()
        plane(2 * index, left_0, right_0)
        total[...] += contract(left_1[...], right_1[...])
        plane(2 * index + 1, left_1, right_1)
        total[...] += contract(left_0[...], right_0[...])
        return carry

    load(0).wait()
    lax.fori_loop(0, cx // 2, pair, 0)
    for face in range(4):
        @pl.when(present[face])
        def _():
            arrival(face, c_source[face], c_halo, c_send, c_recv).wait_recv()
    for face in range(4):
        end = ends[face]
        inner = eps[end] if face < 2 else eps[:, end, :]
        weight = harmonic(inner, permit(c_halo[face], permittivity))
        weight = weight * jnp.where(present[face], 1.0, 0.0)
        for k in range(count):
            value = v[k, end] if face < 2 else v_face[face - 2, k]
            weighted = weight * value
            store_split(left_f, k * cz, weighted, face)
            store_split(own_f, k * cz, value, face)
            if face < 2:
                applied[k, end] += weighted
            else:
                applied[k, :, end, :] += weighted
    total[...] += contract(left_1[...], right_1[...])
    own_block = fold(total[...] + contract(left_f[...], own_f[...]))

    for faces in ((0, 1), (2, 3)):
        for face in faces:
            @pl.when(present[face])
            def _():
                arrival(face, v_source[face], v_halo, v_send, v_recv).wait_recv()
        for face in faces:
            lanes = slice(face * ny, (face + 1) * ny)
            for k in range(count):
                store_split(halo_f, k * cz, v_halo[face, k], face)
            blocks[:, (face + 1) * size:(face + 2) * size] = -fold(
                contract(left_f[:, lanes], halo_f[:, lanes])
            )
    blocks[:, :size] = own_block

    same = (
        lax.broadcasted_iota(jnp.int32, blocks.shape, 0) % cz
        == lax.broadcasted_iota(jnp.int32, blocks.shape, 1) % cz
    )
    kept = jnp.where(same, blocks[...], 0.0).reshape(count, cz, blocks.shape[1])
    kept = jnp.sum(kept, axis=1) * (1.0 / (cz * ny))
    high = kept.astype(jnp.bfloat16).astype(jnp.float32)
    rest = kept - high
    middle = rest.astype(jnp.bfloat16).astype(jnp.float32)
    parts = jnp.concatenate([rest - middle, middle, high], axis=0).astype(jnp.bfloat16)
    placed = jnp.dot(parts, select[...], preferred_element_type=jnp.float32)
    placed = placed[:count] + placed[count:2 * count] + placed[2 * count:]
    for tile in range(nz):
        strip[tile] = placed[:, tile * width:(tile + 1) * width]

    def send_strip(step):
        peer = lax.rem(b + step, nz)
        return pltpu.make_async_remote_copy(
            src_ref=strip.at[peer], dst_ref=rows.at[b], send_sem=strip_send.at[step],
            recv_sem=strip_recv.at[step], device_id=(a, peer), device_id_type=MESH,
        )

    for step in range(1, nz):
        send_strip(step).start()
    rows[b] = strip[b]
    for face in range(4):
        @pl.when(present[face])
        def _():
            copies(face, c_source[face], c_halo, c_send, c_recv).wait_send()
            copies(face, v_source[face], v_halo, v_send, v_recv).wait_send()
    for step in range(1, nz):
        send_strip(step).wait()
    for tile in range(nz):
        coarse[tile * count:(tile + 1) * count, :] = rows[tile, :, :nx * count]


def shards(nx, nz, vectors, classes, permittivity):
    count, cx, cz, ny = vectors.shape
    width = -(-nx * count // LANES) * LANES
    size = count * cz
    f32, i32, bf16 = jnp.float32, jnp.int32, jnp.bfloat16
    dma = pltpu.SemaphoreType.DMA
    vectors, classes, permittivity = (
        pltpu.with_memory_space_constraint(array, pltpu.HBM)
        for array in (vectors, classes, permittivity)
    )
    return pl.pallas_call(
        functools.partial(kernel, nx, nz),
        out_shape=(
            jax.ShapeDtypeStruct(vectors.shape, f32),
            jax.ShapeDtypeStruct((nz * count, nx * count), f32),
        ),
        in_specs=[
            pl.BlockSpec(memory_space=pltpu.HBM),
            pl.BlockSpec(memory_space=pltpu.HBM),
            pl.BlockSpec(memory_space=pltpu.SMEM),
        ],
        out_specs=(
            pl.BlockSpec(memory_space=pltpu.VMEM),
            pl.BlockSpec(memory_space=pltpu.VMEM),
        ),
        scratch_shapes=[
            pltpu.VMEM(vectors.shape, f32),
            pltpu.VMEM(classes.shape, i32),
            pltpu.VMEM(classes.shape, f32),
            pltpu.VMEM((2, cx, ny), i32),
            pltpu.VMEM((2, count, cx, ny), f32),
            pltpu.VMEM((4, cz, ny), i32),
            pltpu.VMEM((4, count, cz, ny), f32),
            pltpu.VMEM((2 * size, ny), bf16),
            pltpu.VMEM((2 * size, ny), bf16),
            pltpu.VMEM((2 * size, ny), bf16),
            pltpu.VMEM((2 * size, ny), bf16),
            pltpu.VMEM((count, cz, ny), f32),
            pltpu.VMEM((2 * size, 4 * ny), bf16),
            pltpu.VMEM((2 * size, 4 * ny), bf16),
            pltpu.VMEM((2 * size, 4 * ny), bf16),
            pltpu.VMEM((2 * size, 2 * size), f32),
            pltpu.VMEM((size, 5 * size), f32),
            pltpu.VMEM((5 * size, nz * width), bf16),
            pltpu.VMEM((nz, count, width), f32),
            pltpu.VMEM((nz, count, width), f32),
            dma((3,)), dma((cx // 2,)), dma((4,)), dma((4,)), dma((4,)), dma((4,)), dma((nz,)), dma((nz,)),
        ],
        compiler_params=pltpu.CompilerParams(
            collective_id=0, has_side_effects=True, vmem_limit_bytes=48 * 2**20
        ),
        cost_estimate=pl.CostEstimate(
            flops=2 * 4 * size * size * cx * ny, bytes_accessed=9 * 2**20, transcendentals=0
        ),
    )(vectors, classes, permittivity)


def solution(mesh):
    return jax.shard_map(
        functools.partial(shards, mesh.shape["gx"], mesh.shape["yz"]),
        mesh=mesh,
        in_specs=(P(None, "gx", "yz", None), P("gx", "yz", None), P()),
        out_specs=(P(None, "gx", "yz", None), P("gx", "yz")),
        check_vma=False,
    )
```

```python
import functools

import jax
import jax.numpy as jnp
from jax import lax
from jax.experimental import pallas as pl
from jax.experimental.pallas import tpu as pltpu
from jax.sharding import PartitionSpec as P

MESH = pl.DeviceIdType.MESH
LANES = 128


def permit(classes, permittivity):
    value = jnp.full(classes.shape, permittivity[0], jnp.float32)
    for index in range(1, permittivity.shape[0]):
        value = jnp.where(classes == index, permittivity[index], value)
    return value


def harmonic(first_value, second_value):
    return 2.0 * first_value * second_value / (first_value + second_value)


def split(value):
    high = value.astype(jnp.bfloat16)
    return high, (value - high.astype(jnp.float32)).astype(jnp.bfloat16)


def contract(left, right):
    return lax.dot_general(
        left, right, (((1,), (1,)), ((), ())), preferred_element_type=jnp.float32
    )


def store_split(target, row, value, face=0):
    rows = target.shape[0] // 2
    size, columns = value.shape
    high, low = split(value)
    lanes = slice(face * columns, (face + 1) * columns)
    target[row:row + size, lanes] = high
    target[rows + row:rows + row + size, lanes] = low


def fold(product):
    rows, columns = product.shape[0] // 2, product.shape[1] // 2
    return (
        product[:rows, :columns]
        + product[:rows, columns:]
        + product[rows:, :columns]
        + product[rows:, columns:]
    )


def kernel(
    nx, nz, v_hbm, c_hbm, permittivity, applied, coarse,
    v, c, eps, c_face, v_face, c_halo, v_halo,
    left_0, right_0, left_1, right_1, flow_x, left_f, own_f, halo_f, total, blocks, select, strip, rows,
    face_sem, load_sem, c_send, c_recv, v_send, v_recv, strip_send, strip_recv,
):
    a, b = lax.axis_index("gx"), lax.axis_index("yz")
    count, cx, cz, ny = v.shape
    width = strip.shape[2]
    neighbour = ((a - 1, b), (a + 1, b), (a, b - 1), (a, b + 1))
    present = (a > 0, a < nx - 1, b > 0, b < nz - 1)

    def load(index):
        part = pl.ds(2 * index, 2)
        return pltpu.make_async_copy(v_hbm.at[:, part], v.at[:, part], load_sem.at[index])

    load_c = pltpu.make_async_copy(c_hbm, c, face_sem.at[0])
    load_low = pltpu.make_async_copy(v_hbm.at[:, :, 0, :], v_face.at[0], face_sem.at[1])
    load_high = pltpu.make_async_copy(v_hbm.at[:, :, cz - 1, :], v_face.at[1], face_sem.at[2])
    load_c.start()
    load_low.start()
    load_high.start()
    for index in range(cx // 2):
        load(index).start()

    barrier = pltpu.get_barrier_semaphore()
    for face in range(2):
        @pl.when(present[face])
        def _():
            pl.semaphore_signal(barrier, inc=1, device_id=neighbour[face], device_id_type=MESH)
    for step in range(1, nz):
        pl.semaphore_signal(
            barrier, inc=1, device_id=(a, lax.rem(b + step, nz)), device_id_type=MESH
        )
    partners = (a > 0).astype(jnp.int32) + (a < nx - 1).astype(jnp.int32) + (nz - 1)

    def copies(face, source, halo, send, recv):
        return pltpu.make_async_remote_copy(
            src_ref=source, dst_ref=halo.at[face ^ 1], send_sem=send.at[face],
            recv_sem=recv.at[face ^ 1], device_id=neighbour[face], device_id_type=MESH,
        )

    def arrival(face, source, halo, send, recv):
        return pltpu.make_async_remote_copy(
            src_ref=source, dst_ref=halo.at[face], send_sem=send.at[face],
            recv_sem=recv.at[face], device_id=neighbour[face], device_id_type=MESH,
        )

    ends = (0, cx - 1, 0, cz - 1)
    c_source = tuple(c_hbm.at[ends[f]] if f < 2 else c_face.at[f - 2] for f in range(4))
    v_source = tuple(v_hbm.at[:, ends[f]] if f < 2 else v_face.at[f - 2] for f in range(4))

    size = count * cz
    s = a * nz + b
    offsets = (0, -nz, nz, -1, 1)
    row = lax.broadcasted_iota(jnp.int32, (size, nz * width), 0) // cz
    column = lax.broadcasted_iota(jnp.int32, (size, nz * width), 1)
    inside = column % width
    target = (column // width) * (nx * count) + inside
    for j in range(5):
        hit = (target == (s + offsets[j]) * count + row) & (inside < nx * count)
        select[j * size:(j + 1) * size] = jnp.where(hit, 1.0, 0.0).astype(jnp.bfloat16)
    total[...] = jnp.zeros_like(total)
    left_1[...] = jnp.zeros_like(left_1)
    right_1[...] = jnp.zeros_like(right_1)
    flow_x[...] = jnp.zeros_like(flow_x)

    load_c.wait()
    for face in (2, 3):
        c_face[face - 2] = c[:, ends[face], :]
    pl.semaphore_wait(barrier, partners)
    for face in (2, 3, 0, 1):
        @pl.when(present[face])
        def _():
            copies(face, c_source[face], c_halo, c_send, c_recv).start()
    load_low.wait()
    for face in (2, 3, 0, 1):
        if face == 3:
            load_high.wait()

        @pl.when(present[face])
        def _():
            copies(face, v_source[face], v_halo, v_send, v_recv).start()

    for x in range(cx):
        eps[x] = permit(c[x], permittivity)
    for face in range(4):
        @pl.when(jnp.logical_not(present[face]))
        def _():
            c_halo[face] = jnp.zeros(c_halo.shape[1:], jnp.int32)
            v_halo[face] = jnp.zeros(v_halo.shape[1:], jnp.float32)

    z_at = lax.broadcasted_iota(jnp.int32, (cz, ny), 0)
    y_at = lax.broadcasted_iota(jnp.int32, (cz, ny), 1)

    def plane(x, left, right):
        after = jnp.minimum(x + 1, cx - 1)
        own = eps[x]
        high_x = harmonic(own, eps[after]) * jnp.where(x < cx - 1, 1.0, 0.0)
        high_z = jnp.where(z_at < cz - 1, harmonic(own, pltpu.roll(own, cz - 1, 0)), 0.0)
        high_y = jnp.where(y_at < ny - 1, harmonic(own, pltpu.roll(own, ny - 1, 1)), 0.0)
        for k in range(count):
            value = v[k, x]
            flow_z = high_z * (value - pltpu.roll(value, cz - 1, 0))
            flow_y = high_y * (value - pltpu.roll(value, ny - 1, 1))
            flow = high_x * (value - v[k, after])
            result = flow - flow_x[k]
            flow_x[k] = flow
            result = result + (flow_z - pltpu.roll(flow_z, 1, 0))
            result = result + (flow_y - pltpu.roll(flow_y, 1, 1))
            applied[k, x] = result
            store_split(left, k * cz, value)
            store_split(right, k * cz, result)

    def pair(index, carry):
        @pl.when(index < cx // 2 - 1)
        def _():
            load(index + 1).wait()
        plane(2 * index, left_0, right_0)
        total[...] += contract(left_1[...], right_1[...])
        plane(2 * index + 1, left_1, right_1)
        total[...] += contract(left_0[...], right_0[...])
        return carry

    load(0).wait()
    lax.fori_loop(0, cx // 2, pair, 0)
    for face in range(4):
        @pl.when(present[face])
        def _():
            arrival(face, c_source[face], c_halo, c_send, c_recv).wait_recv()
    for face in range(4):
        end = ends[face]
        inner = eps[end] if face < 2 else eps[:, end, :]
        weight = harmonic(inner, permit(c_halo[face], permittivity))
        weight = weight * jnp.where(present[face], 1.0, 0.0)
        for k in range(count):
            value = v[k, end] if face < 2 else v_face[face - 2, k]
            weighted = weight * value
            store_split(left_f, k * cz, weighted, face)
            store_split(own_f, k * cz, value, face)
            if face < 2:
                applied[k, end] += weighted
            else:
                applied[k, :, end, :] += weighted
    total[...] += contract(left_1[...], right_1[...])
    own_block = fold(total[...] + contract(left_f[...], own_f[...]))

    for faces in ((0, 1), (2, 3)):
        for face in faces:
            @pl.when(present[face])
            def _():
                arrival(face, v_source[face], v_halo, v_send, v_recv).wait_recv()
        for face in faces:
            lanes = slice(face * ny, (face + 1) * ny)
            for k in range(count):
                store_split(halo_f, k * cz, v_halo[face, k], face)
            blocks[:, (face + 1) * size:(face + 2) * size] = -fold(
                contract(left_f[:, lanes], halo_f[:, lanes])
            )
    blocks[:, :size] = own_block

    same = (
        lax.broadcasted_iota(jnp.int32, blocks.shape, 0) % cz
        == lax.broadcasted_iota(jnp.int32, blocks.shape, 1) % cz
    )
    kept = jnp.where(same, blocks[...], 0.0).reshape(count, cz, blocks.shape[1])
    kept = jnp.sum(kept, axis=1) * (1.0 / (cz * ny))
    high = kept.astype(jnp.bfloat16).astype(jnp.float32)
    rest = kept - high
    middle = rest.astype(jnp.bfloat16).astype(jnp.float32)
    parts = jnp.concatenate([rest - middle, middle, high], axis=0).astype(jnp.bfloat16)
    placed = jnp.dot(parts, select[...], preferred_element_type=jnp.float32)
    placed = placed[:count] + placed[count:2 * count] + placed[2 * count:]
    for tile in range(nz):
        strip[tile] = placed[:, tile * width:(tile + 1) * width]

    def send_strip(step):
        peer = lax.rem(b + step, nz)
        return pltpu.make_async_remote_copy(
            src_ref=strip.at[peer], dst_ref=rows.at[b], send_sem=strip_send.at[step],
            recv_sem=strip_recv.at[step], device_id=(a, peer), device_id_type=MESH,
        )

    for step in range(1, nz):
        send_strip(step).start()
    rows[b] = strip[b]
    for face in range(4):
        @pl.when(present[face])
        def _():
            copies(face, c_source[face], c_halo, c_send, c_recv).wait_send()
            copies(face, v_source[face], v_halo, v_send, v_recv).wait_send()
    for step in range(1, nz):
        send_strip(step).wait()
    for tile in range(nz):
        coarse[tile * count:(tile + 1) * count, :] = rows[tile, :, :nx * count]


def shards(nx, nz, vectors, classes, permittivity):
    count, cx, cz, ny = vectors.shape
    width = -(-nx * count // LANES) * LANES
    size = count * cz
    f32, i32, bf16 = jnp.float32, jnp.int32, jnp.bfloat16
    dma = pltpu.SemaphoreType.DMA
    vectors, classes, permittivity = (
        pltpu.with_memory_space_constraint(array, pltpu.HBM)
        for array in (vectors, classes, permittivity)
    )
    return pl.pallas_call(
        functools.partial(kernel, nx, nz),
        out_shape=(
            jax.ShapeDtypeStruct(vectors.shape, f32),
            jax.ShapeDtypeStruct((nz * count, nx * count), f32),
        ),
        in_specs=[
            pl.BlockSpec(memory_space=pltpu.HBM),
            pl.BlockSpec(memory_space=pltpu.HBM),
            pl.BlockSpec(memory_space=pltpu.SMEM),
        ],
        out_specs=(
            pl.BlockSpec(memory_space=pltpu.VMEM),
            pl.BlockSpec(memory_space=pltpu.VMEM),
        ),
        scratch_shapes=[
            pltpu.VMEM(vectors.shape, f32),
            pltpu.VMEM(classes.shape, i32),
            pltpu.VMEM(classes.shape, f32),
            pltpu.VMEM((2, cx, ny), i32),
            pltpu.VMEM((2, count, cx, ny), f32),
            pltpu.VMEM((4, cz, ny), i32),
            pltpu.VMEM((4, count, cz, ny), f32),
            pltpu.VMEM((2 * size, ny), bf16),
            pltpu.VMEM((2 * size, ny), bf16),
            pltpu.VMEM((2 * size, ny), bf16),
            pltpu.VMEM((2 * size, ny), bf16),
            pltpu.VMEM((count, cz, ny), f32),
            pltpu.VMEM((2 * size, 4 * ny), bf16),
            pltpu.VMEM((2 * size, 4 * ny), bf16),
            pltpu.VMEM((2 * size, 4 * ny), bf16),
            pltpu.VMEM((2 * size, 2 * size), f32),
            pltpu.VMEM((size, 5 * size), f32),
            pltpu.VMEM((5 * size, nz * width), bf16),
            pltpu.VMEM((nz, count, width), f32),
            pltpu.VMEM((nz, count, width), f32),
            dma((3,)), dma((cx // 2,)), dma((4,)), dma((4,)), dma((4,)), dma((4,)), dma((nz,)), dma((nz,)),
        ],
        compiler_params=pltpu.CompilerParams(
            collective_id=0, has_side_effects=True, vmem_limit_bytes=48 * 2**20
        ),
        cost_estimate=pl.CostEstimate(
            flops=2 * 4 * size * size * cx * ny, bytes_accessed=9 * 2**20, transcendentals=0
        ),
    )(vectors, classes, permittivity)


def solution(mesh):
    return jax.shard_map(
        functools.partial(shards, mesh.shape["gx"], mesh.shape["yz"]),
        mesh=mesh,
        in_specs=(P(None, "gx", "yz", None), P("gx", "yz", None), P()),
        out_specs=(P(None, "gx", "yz", None), P("gx", "yz")),
        check_vma=False,
    )
```
